32 devices in a mesh: gx: 2 (over core), gz: 16 (over z, y, x).
Axes of the slice: x: 2, y: 2, z: 4, core: 2. Of those that a mesh axis runs over, the one named last changes fastest.
Arguments:
- modes: bfloat16 [3, 4, 128, 128, 128], P(None, 'gx', None, 'gz'), may hold values from -6 to 6
- weights: float32 [4, 128, 128], P('gx', None, 'gz'), may hold values from 0.0022552917 to 0.022552917
- counts: int32 [32], P(('gx', 'gz')), may hold values from 1 to 128, 1365 in all
- mode_index: int32 [16], replicated, may hold values from 0 to 127, as said below
Outputs:
- slices: float32 [16, 128, 128], P(None, 'gz')
The draws below stay inside these ranges and needn't reach their ends.
Inputs may be any that keep to these rules, and one draw needn't show every extreme that they name: `mode_index`: distinct modes. The counts sum to 128 * 2 * 16 // 3 and one pencil holds 128.
All inputs are finite; a program needn't handle non-finite values. No bound on the sum of `counts` on one device may be relied on, other than what follows from the above.
Results may differ from the reference program's by a relative error of at most 0.004.
Values may be sent and summed in bfloat16 or wider, within the bound.
No kernel may reach another device: no remote copies, remote signals or barrier semaphores. Data moves between devices by JAX's collectives and lax.ppermute only.
A program may use at most 64 MiB of HBM per device.

```python
import math
import jax
import jax.numpy as jnp
import numpy as np
from jax import lax

M = 128
JW = 16
CX = 2
CZ = 8
YCAP = 128
NX = 4
NZ = 128
N_GX = 2
N_GZ = 16
DEVICES = 32


def draw_mode_index(key, part):
    return jax.random.permutation(key, M)[:JW].astype(jnp.int32)


def block_levels(stream_key, extent, cuts, least, top_value):
    gain = 1.0
    for dim, parts in cuts:
        heights = jax.random.uniform(jax.random.fold_in(jax.random.fold_in(stream_key, 6), dim), (parts,), jnp.float32, least / len(cuts), top_value / len(cuts))
        gain = gain * jnp.repeat(jnp.exp(heights), extent[dim] // parts).reshape((-1,) + (1,) * (len(extent) - 1 - dim))
    return gain


def split_up(number_of, total, reach, skew):
    portions = [(1 << 20) // math.isqrt(grade ** skew) + 1 for grade in range(2, number_of + 1)]
    spare, holding = total - reach - (number_of - 1), [1] * (number_of - 1)
    while spare > 0:
        free = [i for i in range(number_of - 1) if holding[i] < reach]
        pool, remaining = sum([portions[i] for i in free]), spare
        for i in free:
            addition = min(reach - holding[i], max(1, remaining * portions[i] // pool), spare)
            holding[i] = holding[i] + addition
            spare = spare - addition
    return np.array([reach] + holding)


def ragged(key, count, total, reach, skew):
    if count == 2:
        one = jax.random.randint(key, (), max(1, total - reach), min(reach, total - 1) + 1)
        return jnp.stack([one, total - one])
    tallies = jnp.asarray(split_up(count, total, reach, skew), jnp.int32)
    couples = (count - 1) // 2
    source_of, taker = tallies[1:1 + 2 * couples:2], tallies[2:2 + 2 * couples:2]
    room = jnp.minimum(source_of - 1, reach - taker)
    shifted = jax.random.randint(jax.random.fold_in(key, 1), (couples,), 0, 1 << 20) % (room + 1)
    tallies = tallies.at[1:1 + 2 * couples:2].set(source_of - shifted).at[2:2 + 2 * couples:2].set(taker + shifted)
    return tallies[jax.random.permutation(jax.random.fold_in(key, 2), count)]


def bell_draw(key, dims, scale, bound, split=(), kind=jnp.bfloat16):
    values = jax.random.normal(key, dims, jnp.float32) * scale
    if len(split) > 0:
        values = block_levels(key, dims, split, -0.22, 0.18) * values
    return jnp.clip(values, min=-bound, max=bound).astype(kind)


def setup_inputs(seed: int = 0) -> dict:
    splits = jax.random.split(jax.random.key(seed), 5)
    return {
        "modes": bell_draw(splits[0], (3, NX, YCAP, NZ, M), 1.0, 6.0, ((1, 2), (3, 16))),
        "weights": jnp.clip(jnp.exp(math.log(0.022552917) - 2.3025851 * jax.random.uniform(splits[1], (NX, YCAP, NZ), jnp.float32) ** block_levels(splits[1], (NX, YCAP, NZ), ((0, 2), (2, 16)), -0.2, 0.2)), 0.0022552917, 0.022552917),
        "counts": ragged(splits[2], N_GX * N_GZ, YCAP * DEVICES // 3, YCAP, 2).astype(jnp.int32),
        "mode_index": draw_mode_index(jax.random.fold_in(splits[4], 71), 0),
    }


def reference(modes, weights, counts, mode_index):
    onehot = (jnp.arange(M)[:, None] == mode_index[None, :]).astype(jnp.float32)
    level_ids = jnp.arange(YCAP, dtype=jnp.int32)
    column_ids = jnp.arange(NZ, dtype=jnp.int32)
    highest = lax.Precision.HIGHEST

    def add_plane(running, x_index):
        behind_index = ((x_index - 1 + NX) % NX).astype(jnp.int32)
        ahead_index = ((x_index + 1) % NX).astype(jnp.int32)
        centre = lax.dynamic_index_in_dim(modes, x_index, 1, keepdims=False).astype(jnp.float32)
        behind = lax.dynamic_index_in_dim(modes, behind_index, 1, keepdims=False).astype(jnp.float32)
        forward = lax.dynamic_index_in_dim(modes, ahead_index, 1, keepdims=False).astype(jnp.float32)
        grad_x = 0.5 * (forward - behind)
        padded = jnp.pad(centre, ((0, 0), (1, 1), (0, 0), (0, 0)))
        grad_y = 0.5 * (padded[:, 2:] - padded[:, :-2])
        grad_z = 0.5 * (jnp.roll(centre, -1, axis=2) - jnp.roll(centre, 1, axis=2))
        gradient = jnp.stack([grad_x, grad_y, grad_z])
        picked = jnp.einsum("cyzm,mj->cyzj", centre, onehot, precision=highest)
        advected = jnp.einsum("dyzj,dcyzk->jcyzk", picked, gradient, precision=highest).astype(jnp.bfloat16)
        pencil = (x_index // CX) * N_GZ + column_ids // CZ
        live_mask = level_ids[:, None] < counts[pencil][None, :]
        weight_row = lax.dynamic_index_in_dim(weights, x_index, 0, keepdims=False)
        weighting = jnp.where(live_mask, weight_row, jnp.zeros_like(weight_row))
        tested = (centre * weighting[None, :, :, None]).astype(jnp.bfloat16)
        contrib = jnp.einsum("cyzi,jcyzk->jik", tested.astype(jnp.float32), advected.astype(jnp.float32), precision=highest)
        return running + contrib, None

    zeroed = jnp.zeros((JW, M, M), jnp.float32)
    slices, unused = lax.scan(add_plane, zeroed, jnp.arange(NX, dtype=jnp.int32))
    return slices
```

```python
import functools

import jax
import jax.numpy as jnp
from jax import lax
from jax.experimental import pallas as pl
from jax.experimental.pallas import tpu as pltpu
from jax.sharding import PartitionSpec as P

LEVELS = 16
UNIT = 16
LANES = 128
VMEM_LIMIT = 48 * 1024 * 1024


def pick_matrix(index_ref, half, comps, size_m):
    lane = lax.broadcasted_iota(jnp.int32, (1, LANES), 1)
    target = jnp.full((1, LANES), -1, jnp.int32)
    for d in range(comps):
        for j in range(half):
            target = jnp.where(lane == d * half + j, index_ref[j] + d * size_m, target)
    row = lax.broadcasted_iota(jnp.int32, (comps * size_m, LANES), 0)
    return jnp.where(row == target, 0.5, 0.0).astype(jnp.bfloat16)


def tested_rows(block, weight_row):
    return (block.astype(jnp.float32).T * weight_row).astype(jnp.bfloat16)


def main_kernel(wrapped, half, span_z, live_ref, index_ref, own_ref, oth_ref, own_w_ref, oth_w_ref, *rest):
    if wrapped:
        acc_ref, pick_ref, picked_ref, adv_ref, test_ref = rest
        edges = ((oth_ref, oth_ref), (own_ref, own_ref))
    else:
        own_edge_ref, oth_edge_ref, acc_ref, pick_ref, picked_ref, adv_ref, test_ref = rest
        edges = ((own_edge_ref, own_edge_ref), (oth_edge_ref, oth_edge_ref))
    comps, span_x, rows, size_m = own_ref.shape
    cap = rows // span_z
    part = LEVELS * span_z
    depth = span_x * part
    per_unit = UNIT // span_z
    pick_ref[...] = pick_matrix(index_ref, half, comps, size_m)
    acc_ref[...] = jnp.zeros_like(acc_ref)
    sub = lax.broadcasted_iota(jnp.int32, (span_z, size_m), 0)

    def plane_refs(which, refs, x):
        body = refs[which]
        other = refs[1 - which]
        if x > 0:
            low = lambda c, r: body[c, x - 1, r]
        elif wrapped:
            low = lambda c, r: other[c, span_x - 1, r]
        else:
            low = lambda c, r: edges[which][0][c, 0, r]
        if x < span_x - 1:
            high = lambda c, r: body[c, x + 1, r]
        elif wrapped:
            high = lambda c, r: other[c, 0, r]
        else:
            high = lambda c, r: edges[which][1][c, 1, r]
        return low, high

    refs = (own_ref, oth_ref)
    weights = (own_w_ref, oth_w_ref)
    for which in range(2):
        body = refs[which]
        live = live_ref[which]

        def block_step(block, carry, which=which, body=body, live=live):
            base = pl.multiple_of(block * part, part)
            spot = pl.ds(base, part)
            wide = []
            for x in range(span_x):
                wide.append(jnp.concatenate([body[d, x, spot] for d in range(comps)], axis=1))
            picked_ref[...] = jnp.dot(
                jnp.concatenate(wide, axis=0), pick_ref[...], preferred_element_type=jnp.float32
            )
            lane = lax.broadcasted_iota(jnp.int32, (1, part), 1)
            mask = (base + lane) < live * span_z
            for x in range(span_x):
                weight_row = jnp.where(mask, weights[which][x, :, spot], 0.0)
                for c in range(comps):
                    test_ref[:, c * depth + x * part : c * depth + (x + 1) * part] = tested_rows(
                        body[c, x, spot], weight_row
                    )
            for x in range(span_x):
                low, high = plane_refs(which, refs, x)

                def unit_step(unit, carry, x=x, low=low, high=high):
                    start = pl.multiple_of(base + unit * UNIT, UNIT)
                    here = pl.ds(start, UNIT)
                    before = pl.ds(pl.multiple_of(jnp.maximum(start - UNIT, 0), UNIT), UNIT)
                    after = pl.ds(pl.multiple_of(jnp.minimum(start + UNIT, rows - UNIT), UNIT), UNIT)
                    has_before = start > 0
                    has_after = start + UNIT < rows
                    grads = []
                    for c in range(comps):
                        mid = body[c, x, here].astype(jnp.float32)
                        down = body[c, x, before].astype(jnp.float32)[UNIT - span_z :]
                        up = body[c, x, after].astype(jnp.float32)[:span_z]
                        down = jnp.where(has_before, down, 0.0)
                        up = jnp.where(has_after, up, 0.0)
                        gx = high(c, here).astype(jnp.float32) - low(c, here).astype(jnp.float32)
                        levels = [down] + [mid[t * span_z : (t + 1) * span_z] for t in range(per_unit)] + [up]
                        for t in range(per_unit):
                            centre = levels[t + 1]
                            gy = levels[t + 2] - levels[t]
                            right = jnp.where(sub == span_z - 1, 0.0, pltpu.roll(centre, span_z - 1, 0))
                            left = jnp.where(sub == 0, 0.0, pltpu.roll(centre, 1, 0))
                            grads.append((gx[t * span_z : (t + 1) * span_z], gy, right - left))
                    local_row = pl.multiple_of(x * part + unit * UNIT, UNIT)
                    picked = picked_ref[pl.ds(local_row, UNIT), :]
                    for j in range(half):
                        outs = [[] for _ in range(comps)]
                        for t in range(per_unit):
                            u = [
                                jnp.broadcast_to(
                                    picked[t * span_z : (t + 1) * span_z, d * half + j : d * half + j + 1],
                                    (span_z, size_m),
                                )
                                for d in range(3)
                            ]
                            for c in range(comps):
                                g = grads[c * per_unit + t]
                                outs[c].append(u[0] * g[0] + u[1] * g[1] + u[2] * g[2])
                        for c in range(comps):
                            value = jnp.concatenate(outs[c], axis=0).astype(jnp.bfloat16)
                            adv_ref[pl.ds(c * depth + local_row, UNIT), j * size_m : (j + 1) * size_m] = value
                    return carry

                lax.fori_loop(0, part // UNIT, unit_step, 0)
            acc_ref[...] += jnp.dot(test_ref[...], adv_ref[...], preferred_element_type=jnp.float32)
            return carry

        lax.fori_loop(0, pl.cdiv(live, LEVELS), block_step, 0)


def seam_kernel(half, index_ref, acc_ref, own_edge_ref, oth_edge_ref, own_last_ref, oth_last_ref, own_w_ref, oth_w_ref, out_ref, adv_ref, total_ref):
    comps, depth, size_m = own_edge_ref.shape
    pieces = out_ref.shape[0]
    owned = size_m // pieces
    pick = pick_matrix(index_ref, half, comps, size_m)[(comps - 1) * size_m :]
    total_ref[...] = acc_ref[...]
    for edge_ref, last_ref, w_ref in (
        (own_edge_ref, own_last_ref, own_w_ref),
        (oth_edge_ref, oth_last_ref, oth_w_ref),
    ):
        for tested_ref, field_ref, w_row, sign in (
            (last_ref, edge_ref, 0, 1.0),
            (edge_ref, last_ref, 1, -1.0),
        ):
            picked = sign * jnp.dot(tested_ref[comps - 1], pick, preferred_element_type=jnp.float32)
            tests = []
            for c in range(comps):
                tests.append(tested_rows(tested_ref[c], w_ref[w_row : w_row + 1, :]))
                field = field_ref[c].astype(jnp.float32)
                for j in range(half):
                    lane = (comps - 1) * half + j
                    adv_ref[c * depth : (c + 1) * depth, j * size_m : (j + 1) * size_m] = (
                        picked[:, lane : lane + 1] * field
                    ).astype(jnp.bfloat16)
            total_ref[...] += jnp.dot(
                jnp.concatenate(tests, axis=1), adv_ref[...], preferred_element_type=jnp.float32
            )
    group = max(1, UNIT // owned)
    for j0 in range(0, half, group):
        parts = [
            total_ref[:, j * size_m : (j + 1) * size_m].reshape(pieces, owned, size_m)
            for j in range(j0, j0 + group)
        ]
        out_ref[:, j0 * owned : (j0 + group) * owned, :] = jnp.concatenate(parts, axis=1).astype(jnp.bfloat16)


def local(modes, weights, counts, mode_index):
    comps, span_x, cap, span_z, size_m = modes.shape
    size_gx, size_gz = lax.axis_size("gx"), lax.axis_size("gz")
    window = mode_index.shape[0]
    half = window // 2
    rows = cap * span_z
    owned = size_m // size_gz
    wrapped = size_gx == 2
    parity = lax.axis_index("gx") % 2
    swap = [(i, i ^ 1) for i in range(size_gx)]
    leftward = [(i, (i - 1) % size_gz) for i in range(size_gz)]

    def other(value):
        return lax.ppermute(value, "gx", swap)

    index_half = lax.dynamic_slice_in_dim(mode_index, parity * half, half)
    own = modes.reshape(comps, span_x, rows, size_m)
    oth = other(own)
    live = jnp.concatenate([counts, other(counts)])
    own_w = weights.reshape(span_x, 1, rows)
    oth_w = other(own_w)
    extra = []
    if not wrapped:
        low = lax.ppermute(own[:, -1:], "gx", [(i, (i + 1) % size_gx) for i in range(size_gx)])
        high = lax.ppermute(own[:, :1], "gx", [(i, (i - 1) % size_gx) for i in range(size_gx)])
        own_edge = jnp.concatenate([low, high], axis=1)
        extra = [own_edge, other(own_edge)]

    masked = jnp.where(jnp.arange(cap)[None, :, None] < counts[0], weights, 0.0)
    depth = span_x * cap
    first = modes[:, :, :, 0].reshape(comps, depth, size_m)
    last = modes[:, :, :, -1].reshape(comps, depth, size_m)
    edge = lax.ppermute(first, "gz", leftward)
    edge_w = lax.ppermute(masked[:, :, 0].reshape(1, depth), "gz", leftward)
    seam_w = jnp.concatenate([masked[:, :, -1].reshape(1, depth), edge_w])

    vmem = pl.BlockSpec(memory_space=pltpu.VMEM)
    smem = pl.BlockSpec(memory_space=pltpu.SMEM)
    block_depth = comps * span_x * LEVELS * span_z
    acc = pl.pallas_call(
        functools.partial(main_kernel, wrapped, half, span_z),
        out_shape=jax.ShapeDtypeStruct((size_m, half * size_m), jnp.float32),
        in_specs=[smem, smem] + [vmem] * (4 + len(extra)),
        out_specs=vmem,
        scratch_shapes=[
            pltpu.VMEM((comps * size_m, LANES), jnp.bfloat16),
            pltpu.VMEM((block_depth // comps, LANES), jnp.float32),
            pltpu.VMEM((block_depth, half * size_m), jnp.bfloat16),
            pltpu.VMEM((size_m, block_depth), jnp.bfloat16),
        ],
        compiler_params=pltpu.CompilerParams(vmem_limit_bytes=VMEM_LIMIT),
    )(live, index_half, own, oth, own_w, oth_w, *extra)

    partial = pl.pallas_call(
        functools.partial(seam_kernel, half),
        out_shape=jax.ShapeDtypeStruct((size_gz, half * owned, size_m), jnp.bfloat16),
        in_specs=[smem] + [vmem] * 7,
        out_specs=vmem,
        scratch_shapes=[
            pltpu.VMEM((comps * depth, half * size_m), jnp.bfloat16),
            pltpu.VMEM((size_m, half * size_m), jnp.float32),
        ],
        compiler_params=pltpu.CompilerParams(vmem_limit_bytes=VMEM_LIMIT),
    )(index_half, acc, edge, other(edge), last, other(last), seam_w, other(seam_w))

    pieces = lax.all_to_all(partial, "gz", 0, 0, tiled=True)
    mine = pieces.astype(jnp.float32).sum(axis=0)
    if wrapped:
        theirs = other(mine)
        both = jnp.where(parity == 0, jnp.stack([mine, theirs]), jnp.stack([theirs, mine]))
    else:
        both = lax.psum(
            jnp.where(jnp.arange(2)[:, None, None] == parity, mine[None], 0.0), "gx"
        )
    return both.reshape(window, owned, size_m)


def solution(mesh):
    placed = (P(None, "gx", None, "gz", None), P("gx", None, "gz"), P(("gx", "gz")), P())
    return jax.shard_map(
        local, mesh=mesh, in_specs=placed, out_specs=P(None, "gz", None), check_vma=False
    )
```

```python
import functools

import jax
import jax.numpy as jnp
from jax import lax
from jax.experimental import pallas as pl
from jax.experimental.pallas import tpu as pltpu
from jax.sharding import PartitionSpec as P

LANES = 128
PACKED = 16
GROUP = 4
SPLITS = 3
VMEM_LIMIT = 48 * 1024 * 1024


def pick_matrix(index_ref, half, comps, size_m):
    offset = (lax.axis_index("gx") % 2) * half
    lane = lax.broadcasted_iota(jnp.int32, (1, LANES), 1)
    target = jnp.full((1, LANES), -1, jnp.int32)
    for d in range(comps):
        for j in range(half):
            target = jnp.where(lane == d * half + j, index_ref[offset + j] + d * size_m, target)
    row = lax.broadcasted_iota(jnp.int32, (comps * size_m, LANES), 0)
    return jnp.where(row == target, 0.5, 0.0).astype(jnp.bfloat16)


def split_parts(value):
    parts = []
    for _ in range(SPLITS):
        part = value.astype(jnp.bfloat16)
        parts.append(part)
        value = value - part.astype(jnp.float32)
    return parts


def pack_kernel(counts_ref, own_ref, weight_ref, row_ref, first_ref, last_ref, near_ref, near_w_ref, wide_ref, sems, w_sem):
    comps, span_x, rows, size_m = own_ref.shape
    span_z, cap = weight_ref.shape[1:]
    depth = span_x * cap
    copy_w = pltpu.make_async_copy(weight_ref, near_w_ref, w_sem)
    copy_w.start()
    planes = [(c, x) for c in range(comps) for x in range(span_x)]
    copies = []
    for n, (c, x) in enumerate(planes):
        copy = pltpu.make_async_copy(own_ref.at[c, x], near_ref.at[c, x], sems.at[n])
        copy.start()
        copies.append(copy)
    live = counts_ref[0]
    level = lax.broadcasted_iota(jnp.int32, (span_z, cap), 1)
    spread = (
        lax.broadcasted_iota(jnp.int32, (cap, rows), 0) == lax.broadcasted_iota(jnp.int32, (cap, rows), 1) // span_z
    ).astype(jnp.bfloat16)
    column = lax.broadcasted_iota(jnp.int32, (span_z, rows), 1) % span_z
    mine = column == lax.broadcasted_iota(jnp.int32, (span_z, rows), 0)
    firsts, lasts = [], []
    copy_w.wait()
    for x in range(span_x):
        weight = jnp.where(level < live, near_w_ref[x], 0.0)
        parts = split_parts(weight)
        wide = jnp.dot(jnp.concatenate(parts, axis=0), spread, preferred_element_type=jnp.float32)
        total = wide[:span_z]
        for s in range(1, SPLITS):
            total = total + wide[s * span_z : (s + 1) * span_z]
        row_ref[x] = jnp.sum(jnp.where(mine, total, 0.0), axis=0, keepdims=True)
        firsts += [part[:1] for part in parts]
        lasts += [part[span_z - 1 :] for part in parts]
    filler = jnp.zeros((PACKED - SPLITS * span_x, cap), jnp.bfloat16)
    for out_ref, pieces in ((first_ref, firsts), (last_ref, lasts)):
        out_ref[comps * depth :, :] = jnp.concatenate(pieces + [filler], axis=0)
    for copy, (c, x) in zip(copies, planes):
        copy.wait()
        wide_ref[c, x] = near_ref[c, x].astype(jnp.float32)
        start = c * depth + x * cap
        for out_ref, z in ((first_ref, 0), (last_ref, span_z - 1)):
            out_ref[start : start + cap, :] = wide_ref[c, x, pl.ds(z, cap, stride=span_z), :].astype(jnp.bfloat16)


def main_kernel(wrapped, half, span_z, own_live_ref, oth_live_ref, index_ref, own_ref, oth_ref, own_w_ref, oth_w_ref, *rest):
    edges = () if wrapped else rest[:2]
    acc_ref, pick_ref, picked_ref, grad_ref, low_ref, high_ref, test_ref, next_ref = rest[-8:]
    comps, span_x, rows, size_m = own_ref.shape
    part = LANES
    levels = part // span_z
    depth = span_x * part
    margin = 2 * span_z
    middle = half // 2
    refs = (own_ref, oth_ref)
    weights = (own_w_ref, oth_w_ref)
    column = lax.broadcasted_iota(jnp.int32, (1, span_z, size_m), 1)

    def neighbours(which, x):
        body, other = refs[which], refs[1 - which]
        if x > 0:
            low = (body, x - 1)
        else:
            low = (other, span_x - 1) if wrapped else (edges[which], 0)
        if x < span_x - 1:
            high = (body, x + 1)
        else:
            high = (other, 0) if wrapped else (edges[which], 1)
        return low, high

    def prepare(which, block):
        body = refs[which]
        base = pl.multiple_of(block * part, part)
        spot = pl.ds(base, part)
        before = pl.ds(pl.multiple_of(jnp.maximum(base - margin, 0), margin), margin)
        after = pl.ds(pl.multiple_of(jnp.minimum(base + part, rows - margin), margin), margin)
        wide = [jnp.concatenate([body[d, x, spot] for d in range(comps)], axis=1) for x in range(span_x)]
        picked = jnp.dot(jnp.concatenate(wide, axis=0), pick_ref[...], preferred_element_type=jnp.float32)
        for x in range(span_x):
            weight = jnp.broadcast_to(weights[which][x, :, spot], (part, part)).T
            low, high = neighbours(which, x)
            for c in range(comps):
                mid = body[c, x, spot].astype(jnp.float32)
                row = c * depth + x * part
                next_ref[row : row + part, :] = (mid * weight).astype(jnp.bfloat16)
                gx = high[0][c, high[1], spot].astype(jnp.float32) - low[0][c, low[1], spot].astype(jnp.float32)
                grad_ref[x, c] = gx.T
                down = jnp.where(base > 0, body[c, x, before].astype(jnp.float32)[margin - span_z :], 0.0)
                up = jnp.where(base + part < rows, body[c, x, after].astype(jnp.float32)[:span_z], 0.0)
                gy = jnp.concatenate([mid[span_z:], up], axis=0) - jnp.concatenate([down, mid[: part - span_z]], axis=0)
                grad_ref[x, comps + c] = gy.T
                mid = mid.reshape(levels, span_z, size_m)
                right = jnp.where(column == span_z - 1, 0.0, pltpu.roll(mid, span_z - 1, 1))
                left = jnp.where(column == 0, 0.0, pltpu.roll(mid, 1, 1))
                grad_ref[x, 2 * comps + c] = (right - left).reshape(part, size_m).T
        for x in range(span_x):
            picked_ref[x] = picked[x * part : (x + 1) * part].T

    def advect(first, last, adv_ref):
        for x in range(span_x):
            for j0 in range(first, last, GROUP):
                group = range(j0, min(j0 + GROUP, last))
                u = [
                    [jnp.broadcast_to(picked_ref[x, d * half + j : d * half + j + 1, :], (PACKED, part)) for d in range(3)]
                    for j in group
                ]
                for k in range(0, size_m, PACKED):
                    g = [grad_ref[x, n, k : k + PACKED, :] for n in range(3 * comps)]
                    for t, j in enumerate(group):
                        for c in range(comps):
                            value = u[t][0] * g[c] + u[t][1] * g[comps + c] + u[t][2] * g[2 * comps + c]
                            row = (j - first) * size_m + k
                            col = c * depth + x * part
                            adv_ref[row : row + PACKED, col : col + part] = value.astype(jnp.bfloat16)

    def contract(first, last, adv_ref):
        some = slice(first * size_m, last * size_m)
        acc_ref[some, :] += jnp.dot(adv_ref[...], test_ref[...], preferred_element_type=jnp.float32)

    pick_ref[...] = pick_matrix(index_ref, half, comps, size_m)
    acc_ref[...] = jnp.zeros_like(acc_ref)
    test_ref[...] = jnp.zeros_like(test_ref)
    high_ref[...] = jnp.zeros_like(high_ref)
    for which, live_ref in ((0, own_live_ref), (1, oth_live_ref)):
        prepare(which, 0)

        def block_step(block, carry, which=which):
            contract(middle, half, high_ref)
            advect(0, middle, low_ref)
            test_ref[...] = next_ref[...]
            contract(0, middle, low_ref)
            advect(middle, half, high_ref)
            prepare(which, jnp.minimum(block + 1, rows // part - 1))
            return carry

        lax.fori_loop(0, pl.cdiv(live_ref[0], levels), block_step, 0)
    contract(middle, half, high_ref)


def seam_kernel(half, span_x, comps, final, index_ref, acc_ref, edge_ref, last_ref, out_ref, adv_ref, test_ref, picked_ref, *rest):
    size_m = acc_ref.shape[1]
    part = LANES
    depth = span_x * part
    body = comps * depth
    total_ref = rest[0] if final else out_ref
    pick = pick_matrix(index_ref, half, comps, size_m)[(comps - 1) * size_m :]
    update = acc_ref[...]
    for tested_ref, field_ref, sign in ((last_ref, edge_ref, 1.0), (edge_ref, last_ref, -1.0)):
        third = tested_ref[(comps - 1) * depth : body, :]
        picked = sign * jnp.dot(third, pick, preferred_element_type=jnp.float32)
        splits = tested_ref[body:, :].astype(jnp.float32)
        for x in range(span_x):
            row = sum(splits[x * SPLITS + s : x * SPLITS + s + 1] for s in range(SPLITS))
            weight = jnp.broadcast_to(row, (part, part)).T
            picked_ref[x] = picked[x * part : (x + 1) * part].T
            for c in range(comps):
                spot = slice(c * depth + x * part, c * depth + (x + 1) * part)
                test_ref[spot, :] = (tested_ref[spot, :].astype(jnp.float32) * weight).astype(jnp.bfloat16)
                field = field_ref[spot, :].astype(jnp.float32).T
                for j in range(half):
                    lane = (comps - 1) * half + j
                    adv_ref[j * size_m : (j + 1) * size_m, spot] = (field * picked_ref[x, lane : lane + 1, :]).astype(
                        jnp.bfloat16
                    )
        update = update + jnp.dot(adv_ref[...], test_ref[...], preferred_element_type=jnp.float32)
        total_ref[...] = update
        update = total_ref[...]
    if final:
        pieces = out_ref.shape[0]
        owned = size_m // pieces
        group = max(1, PACKED // owned)
        for j0 in range(0, half, group):
            parts = [
                total_ref[j * size_m : (j + 1) * size_m, :].T.reshape(pieces, owned, size_m)
                for j in range(j0, j0 + group)
            ]
            out_ref[:, j0 * owned : (j0 + group) * owned, :] = jnp.concatenate(parts, axis=1).astype(jnp.bfloat16)


def local(modes, weights, counts, mode_index):
    comps, span_x, cap, span_z, size_m = modes.shape
    size_gx, size_gz = lax.axis_size("gx"), lax.axis_size("gz")
    window = mode_index.shape[0]
    half = window // 2
    rows = cap * span_z
    depth = span_x * cap
    owned = size_m // size_gz
    wrapped = size_gx == 2
    parity = lax.axis_index("gx") % 2
    swap = [(i, i ^ 1) for i in range(size_gx)]
    leftward = [(i, (i - 1) % size_gz) for i in range(size_gz)]
    vmem = pl.BlockSpec(memory_space=pltpu.VMEM)
    smem = pl.BlockSpec(memory_space=pltpu.SMEM)
    anywhere = pl.BlockSpec(memory_space=pltpu.HBM)
    params = pltpu.CompilerParams(vmem_limit_bytes=VMEM_LIMIT)

    def other(value):
        return lax.ppermute(value, "gx", swap)

    own = modes.reshape(comps, span_x, rows, size_m)
    oth = other(own)
    oth_counts = other(counts)
    extra = []
    if not wrapped:
        low = lax.ppermute(own[:, -1:], "gx", [(i, (i + 1) % size_gx) for i in range(size_gx)])
        high = lax.ppermute(own[:, :1], "gx", [(i, (i - 1) % size_gx) for i in range(size_gx)])
        own_edge = jnp.concatenate([low, high], axis=1)
        extra = [own_edge, other(own_edge)]

    column = jax.ShapeDtypeStruct((comps * depth + PACKED, size_m), jnp.bfloat16)
    own_w, first, last = pl.pallas_call(
        pack_kernel,
        out_shape=[jax.ShapeDtypeStruct((span_x, 1, rows), jnp.float32), column, column],
        in_specs=[smem, anywhere, anywhere],
        out_specs=[vmem] * 3,
        scratch_shapes=[
            pltpu.VMEM((comps, span_x, rows, size_m), jnp.bfloat16),
            pltpu.VMEM((span_x, span_z, cap), jnp.float32),
            pltpu.VMEM((comps, span_x, rows, size_m), jnp.float32),
            pltpu.SemaphoreType.DMA((comps * span_x,)),
            pltpu.SemaphoreType.DMA,
        ],
        compiler_params=params,
    )(counts, own, weights.transpose(0, 2, 1))
    edge = lax.ppermute(first, "gz", leftward)
    oth_w = other(own_w)
    oth_last = other(last)

    block_depth = comps * span_x * LANES
    acc = pl.pallas_call(
        functools.partial(main_kernel, wrapped, half, span_z),
        out_shape=jax.ShapeDtypeStruct((half * size_m, size_m), jnp.float32),
        in_specs=[smem] * 3 + [vmem] * (4 + len(extra)),
        out_specs=vmem,
        scratch_shapes=[
            pltpu.VMEM((comps * size_m, LANES), jnp.bfloat16),
            pltpu.VMEM((span_x, LANES, LANES), jnp.float32),
            pltpu.VMEM((span_x, 3 * comps, size_m, LANES), jnp.float32),
            pltpu.VMEM((half // 2 * size_m, block_depth), jnp.bfloat16),
            pltpu.VMEM(((half - half // 2) * size_m, block_depth), jnp.bfloat16),
            pltpu.VMEM((block_depth, size_m), jnp.bfloat16),
            pltpu.VMEM((block_depth, size_m), jnp.bfloat16),
        ],
        compiler_params=params,
        cost_estimate=pl.CostEstimate(
            flops=4 * comps * depth * span_z * half * size_m * size_m, bytes_accessed=4 * own.size, transcendentals=0
        ),
    )(counts, oth_counts, mode_index, own, oth, own_w, oth_w, *extra)

    acc, edge = lax.optimization_barrier((acc, edge))
    oth_edge = other(edge)
    seam_scratch = [
        pltpu.VMEM((half * size_m, comps * depth), jnp.bfloat16),
        pltpu.VMEM((comps * depth, size_m), jnp.bfloat16),
        pltpu.VMEM((span_x, LANES, LANES), jnp.float32),
    ]
    acc = pl.pallas_call(
        functools.partial(seam_kernel, half, span_x, comps, False),
        out_shape=jax.ShapeDtypeStruct(acc.shape, jnp.float32),
        in_specs=[smem] + [vmem] * 3,
        out_specs=vmem,
        scratch_shapes=seam_scratch,
        compiler_params=params,
        cost_estimate=pl.CostEstimate(
            flops=4 * comps * depth * half * size_m * size_m, bytes_accessed=4 * own.size, transcendentals=0
        ),
    )(mode_index, acc, edge, last)
    partial = pl.pallas_call(
        functools.partial(seam_kernel, half, span_x, comps, True),
        out_shape=jax.ShapeDtypeStruct((size_gz, half * owned, size_m), jnp.bfloat16),
        in_specs=[smem] + [vmem] * 3,
        out_specs=vmem,
        scratch_shapes=seam_scratch + [pltpu.VMEM(acc.shape, jnp.float32)],
        compiler_params=params,
    )(mode_index, acc, oth_edge, oth_last)

    pieces = lax.all_to_all(partial, "gz", 0, 0, tiled=True)
    mine = pieces.astype(jnp.float32).sum(axis=0)
    if wrapped:
        theirs = other(mine)
        both = jnp.where(parity == 0, jnp.stack([mine, theirs]), jnp.stack([theirs, mine]))
    else:
        both = lax.psum(jnp.where(jnp.arange(2)[:, None, None] == parity, mine[None], 0.0), "gx")
    return both.reshape(window, owned, size_m)


def solution(mesh):
    placed = (P(None, "gx", None, "gz", None), P("gx", None, "gz"), P(("gx", "gz")), P())
    return jax.shard_map(
        local, mesh=mesh, in_specs=placed, out_specs=P(None, "gz", None), check_vma=False
    )
```

```python
import functools

import jax
import jax.numpy as jnp
from jax import lax
from jax.experimental import pallas as pl
from jax.experimental.pallas import tpu as pltpu
from jax.sharding import PartitionSpec as P

LANES = 128
PACKED = 16
GROUP = 2
SPLITS = 3
VMEM_LIMIT = 48 * 1024 * 1024


def pick_matrix(index_ref, half, comps, size_m):
    offset = (lax.axis_index("gx") % 2) * half
    lane = lax.broadcasted_iota(jnp.int32, (1, LANES), 1)
    target = jnp.full((1, LANES), -1, jnp.int32)
    for d in range(comps):
        for j in range(half):
            target = jnp.where(lane == d * half + j, index_ref[offset + j] + d * size_m, target)
    row = lax.broadcasted_iota(jnp.int32, (comps * size_m, LANES), 0)
    return jnp.where(row == target, 0.5, 0.0).astype(jnp.bfloat16)


def split_parts(value):
    parts = []
    for _ in range(SPLITS):
        part = value.astype(jnp.bfloat16)
        parts.append(part)
        value = value - part.astype(jnp.float32)
    return parts


def pack_kernel(counts_ref, own_ref, weight_ref, row_ref, first_ref, last_ref, near_ref, near_w_ref, wide_ref, sems, w_sem):
    comps, span_x, rows, size_m = own_ref.shape
    span_z, cap = weight_ref.shape[1:]
    depth = span_x * cap
    copy_w = pltpu.make_async_copy(weight_ref, near_w_ref, w_sem)
    copy_w.start()
    planes = [(c, x) for c in range(comps) for x in range(span_x)]
    copies = []
    for n, (c, x) in enumerate(planes):
        copy = pltpu.make_async_copy(own_ref.at[c, x], near_ref.at[c, x], sems.at[n])
        copy.start()
        copies.append(copy)
    live = counts_ref[0]
    level = lax.broadcasted_iota(jnp.int32, (span_z, cap), 1)
    spread = (
        lax.broadcasted_iota(jnp.int32, (cap, rows), 0) == lax.broadcasted_iota(jnp.int32, (cap, rows), 1) // span_z
    ).astype(jnp.bfloat16)
    column = lax.broadcasted_iota(jnp.int32, (span_z, rows), 1) % span_z
    mine = column == lax.broadcasted_iota(jnp.int32, (span_z, rows), 0)
    firsts, lasts = [], []
    copy_w.wait()
    for x in range(span_x):
        weight = jnp.where(level < live, near_w_ref[x], 0.0)
        parts = split_parts(weight)
        wide = jnp.dot(jnp.concatenate(parts, axis=0), spread, preferred_element_type=jnp.float32)
        total = wide[:span_z]
        for s in range(1, SPLITS):
            total = total + wide[s * span_z : (s + 1) * span_z]
        row_ref[x] = jnp.sum(jnp.where(mine, total, 0.0), axis=0, keepdims=True)
        firsts += [part[:1] for part in parts]
        lasts += [part[span_z - 1 :] for part in parts]
    filler = jnp.zeros((PACKED - SPLITS * span_x, cap), jnp.bfloat16)
    for out_ref, pieces in ((first_ref, firsts), (last_ref, lasts)):
        out_ref[comps * depth :, :] = jnp.concatenate(pieces + [filler], axis=0)
    for copy, (c, x) in zip(copies, planes):
        copy.wait()
        wide_ref[c, x] = near_ref[c, x].astype(jnp.float32)
        start = c * depth + x * cap
        for out_ref, z in ((first_ref, 0), (last_ref, span_z - 1)):
            out_ref[start : start + cap, :] = wide_ref[c, x, pl.ds(z, cap, stride=span_z), :].astype(jnp.bfloat16)


def main_kernel(wrapped, half, span_z, own_live_ref, oth_live_ref, index_ref, own_ref, oth_ref, own_w_ref, oth_w_ref, *rest):
    edges = () if wrapped else rest[:2]
    acc_ref, pick_ref, picked_ref, grad_ref, low_ref, high_ref, test_ref, next_ref = rest[-8:]
    comps, span_x, rows, size_m = own_ref.shape
    part = LANES
    levels = part // span_z
    depth = span_x * part
    margin = 2 * span_z
    middle = half // 2
    refs = (own_ref, oth_ref)
    weights = (own_w_ref, oth_w_ref)
    column = lax.broadcasted_iota(jnp.int32, (1, span_z, size_m), 1)

    def neighbours(which, x):
        body, other = refs[which], refs[1 - which]
        if x > 0:
            low = (body, x - 1)
        else:
            low = (other, span_x - 1) if wrapped else (edges[which], 0)
        if x < span_x - 1:
            high = (body, x + 1)
        else:
            high = (other, 0) if wrapped else (edges[which], 1)
        return low, high

    def prepare(which, block):
        body = refs[which]
        base = pl.multiple_of(block * part, part)
        spot = pl.ds(base, part)
        before = pl.ds(pl.multiple_of(jnp.maximum(base - margin, 0), margin), margin)
        after = pl.ds(pl.multiple_of(jnp.minimum(base + part, rows - margin), margin), margin)
        wide = [jnp.concatenate([body[d, x, spot] for d in range(comps)], axis=1) for x in range(span_x)]
        picked = jnp.dot(jnp.concatenate(wide, axis=0), pick_ref[...], preferred_element_type=jnp.float32)
        for x in range(span_x):
            weight = jnp.broadcast_to(weights[which][x, :, spot], (part, part)).T
            low, high = neighbours(which, x)
            for c in range(comps):
                mid = body[c, x, spot].astype(jnp.float32)
                row = c * depth + x * part
                next_ref[row : row + part, :] = (mid * weight).astype(jnp.bfloat16)
                gx = high[0][c, high[1], spot].astype(jnp.float32) - low[0][c, low[1], spot].astype(jnp.float32)
                grad_ref[x, c] = gx.T
                down = jnp.where(base > 0, body[c, x, before].astype(jnp.float32)[margin - span_z :], 0.0)
                up = jnp.where(base + part < rows, body[c, x, after].astype(jnp.float32)[:span_z], 0.0)
                gy = jnp.concatenate([mid[span_z:], up], axis=0) - jnp.concatenate([down, mid[: part - span_z]], axis=0)
                grad_ref[x, comps + c] = gy.T
                mid = mid.reshape(levels, span_z, size_m)
                right = jnp.where(column == span_z - 1, 0.0, pltpu.roll(mid, span_z - 1, 1))
                left = jnp.where(column == 0, 0.0, pltpu.roll(mid, 1, 1))
                grad_ref[x, 2 * comps + c] = (right - left).reshape(part, size_m).T
        for x in range(span_x):
            picked_ref[x] = picked[x * part : (x + 1) * part].T

    def advect(first, last, adv_ref):
        for j0 in range(first, last, GROUP):
            group = range(j0, min(j0 + GROUP, last))
            u = [
                [
                    [jnp.broadcast_to(picked_ref[x, d * half + j : d * half + j + 1, :], (PACKED, part)) for d in range(3)]
                    for x in range(span_x)
                ]
                for j in group
            ]
            for k in range(0, size_m, PACKED):
                for c in range(comps):
                    g = [[grad_ref[x, d * comps + c, k : k + PACKED, :] for d in range(3)] for x in range(span_x)]
                    for t, j in enumerate(group):
                        value = jnp.concatenate(
                            [u[t][x][0] * g[x][0] + u[t][x][1] * g[x][1] + u[t][x][2] * g[x][2] for x in range(span_x)],
                            axis=1,
                        )
                        row = (j - first) * size_m + k
                        adv_ref[row : row + PACKED, c * depth : (c + 1) * depth] = value.astype(jnp.bfloat16)

    def contract(first, last, adv_ref):
        some = slice(first * size_m, last * size_m)
        acc_ref[some, :] += jnp.dot(adv_ref[...], test_ref[...], preferred_element_type=jnp.float32)

    pick_ref[...] = pick_matrix(index_ref, half, comps, size_m)
    acc_ref[...] = jnp.zeros_like(acc_ref)
    test_ref[...] = jnp.zeros_like(test_ref)
    high_ref[...] = jnp.zeros_like(high_ref)
    def block_step(ahead):
        contract(middle, half, high_ref)
        advect(0, middle, low_ref)
        test_ref[...] = next_ref[...]
        contract(0, middle, low_ref)
        advect(middle, half, high_ref)
        if ahead is not None:
            prepare(*ahead)

    def blocks_but_last(which, live_ref):
        def step(block, carry):
            block_step((which, block + 1))
            return carry

        lax.fori_loop(0, pl.cdiv(live_ref[0], levels) - 1, step, 0)

    prepare(0, 0)
    blocks_but_last(0, own_live_ref)
    block_step((1, 0))
    blocks_but_last(1, oth_live_ref)
    block_step(None)
    contract(middle, half, high_ref)


def seam_kernel(half, span_x, comps, final, index_ref, acc_ref, edge_ref, last_ref, out_ref, adv_ref, test_ref, picked_ref, *rest):
    size_m = acc_ref.shape[1]
    part = LANES
    depth = span_x * part
    body = comps * depth
    total_ref = rest[0] if final else out_ref
    pick = pick_matrix(index_ref, half, comps, size_m)[(comps - 1) * size_m :]
    update = acc_ref[...]
    for tested_ref, field_ref, sign in ((last_ref, edge_ref, 1.0), (edge_ref, last_ref, -1.0)):
        third = tested_ref[(comps - 1) * depth : body, :]
        picked = sign * jnp.dot(third, pick, preferred_element_type=jnp.float32)
        splits = tested_ref[body:, :].astype(jnp.float32)
        for x in range(span_x):
            row = sum(splits[x * SPLITS + s : x * SPLITS + s + 1] for s in range(SPLITS))
            weight = jnp.broadcast_to(row, (part, part)).T
            picked_ref[x] = picked[x * part : (x + 1) * part].T
            for c in range(comps):
                spot = slice(c * depth + x * part, c * depth + (x + 1) * part)
                test_ref[spot, :] = (tested_ref[spot, :].astype(jnp.float32) * weight).astype(jnp.bfloat16)
        for c in range(comps):
            spots = [slice(c * depth + x * part, c * depth + (x + 1) * part) for x in range(span_x)]
            fields = [field_ref[spot, :].astype(jnp.float32).T for spot in spots]
            for j in range(half):
                lane = (comps - 1) * half + j
                value = jnp.concatenate([fields[x] * picked_ref[x, lane : lane + 1, :] for x in range(span_x)], axis=1)
                adv_ref[j * size_m : (j + 1) * size_m, c * depth : (c + 1) * depth] = value.astype(jnp.bfloat16)
        update = update + jnp.dot(adv_ref[...], test_ref[...], preferred_element_type=jnp.float32)
        total_ref[...] = update
        update = total_ref[...]
    if final:
        pieces = out_ref.shape[0]
        owned = size_m // pieces
        group = max(1, PACKED // owned)
        for j0 in range(0, half, group):
            parts = [
                total_ref[j * size_m : (j + 1) * size_m, :].T.reshape(pieces, owned, size_m)
                for j in range(j0, j0 + group)
            ]
            out_ref[:, j0 * owned : (j0 + group) * owned, :] = jnp.concatenate(parts, axis=1).astype(jnp.bfloat16)


def local(modes, weights, counts, mode_index):
    comps, span_x, cap, span_z, size_m = modes.shape
    size_gx, size_gz = lax.axis_size("gx"), lax.axis_size("gz")
    window = mode_index.shape[0]
    half = window // 2
    rows = cap * span_z
    depth = span_x * cap
    owned = size_m // size_gz
    wrapped = size_gx == 2
    parity = lax.axis_index("gx") % 2
    swap = [(i, i ^ 1) for i in range(size_gx)]
    leftward = [(i, (i - 1) % size_gz) for i in range(size_gz)]
    vmem = pl.BlockSpec(memory_space=pltpu.VMEM)
    smem = pl.BlockSpec(memory_space=pltpu.SMEM)
    anywhere = pl.BlockSpec(memory_space=pltpu.HBM)
    params = pltpu.CompilerParams(vmem_limit_bytes=VMEM_LIMIT)

    def other(value):
        return lax.ppermute(value, "gx", swap)

    own = modes.reshape(comps, span_x, rows, size_m)
    oth = other(own)
    oth_counts = other(counts)
    extra = []
    if not wrapped:
        low = lax.ppermute(own[:, -1:], "gx", [(i, (i + 1) % size_gx) for i in range(size_gx)])
        high = lax.ppermute(own[:, :1], "gx", [(i, (i - 1) % size_gx) for i in range(size_gx)])
        own_edge = jnp.concatenate([low, high], axis=1)
        extra = [own_edge, other(own_edge)]

    column = jax.ShapeDtypeStruct((comps * depth + PACKED, size_m), jnp.bfloat16)
    own_w, first, last = pl.pallas_call(
        pack_kernel,
        out_shape=[jax.ShapeDtypeStruct((span_x, 1, rows), jnp.float32), column, column],
        in_specs=[smem, anywhere, anywhere],
        out_specs=[vmem] * 3,
        scratch_shapes=[
            pltpu.VMEM((comps, span_x, rows, size_m), jnp.bfloat16),
            pltpu.VMEM((span_x, span_z, cap), jnp.float32),
            pltpu.VMEM((comps, span_x, rows, size_m), jnp.float32),
            pltpu.SemaphoreType.DMA((comps * span_x,)),
            pltpu.SemaphoreType.DMA,
        ],
        compiler_params=params,
    )(counts, own, weights.transpose(0, 2, 1))
    edge = lax.ppermute(first, "gz", leftward)
    oth_w = other(own_w)
    oth_last = other(last)

    block_depth = comps * span_x * LANES
    acc = pl.pallas_call(
        functools.partial(main_kernel, wrapped, half, span_z),
        out_shape=jax.ShapeDtypeStruct((half * size_m, size_m), jnp.float32),
        in_specs=[smem] * 3 + [vmem] * (4 + len(extra)),
        out_specs=vmem,
        scratch_shapes=[
            pltpu.VMEM((comps * size_m, LANES), jnp.bfloat16),
            pltpu.VMEM((span_x, LANES, LANES), jnp.float32),
            pltpu.VMEM((span_x, 3 * comps, size_m, LANES), jnp.float32),
            pltpu.VMEM((half // 2 * size_m, block_depth), jnp.bfloat16),
            pltpu.VMEM(((half - half // 2) * size_m, block_depth), jnp.bfloat16),
            pltpu.VMEM((block_depth, size_m), jnp.bfloat16),
            pltpu.VMEM((block_depth, size_m), jnp.bfloat16),
        ],
        compiler_params=params,
        cost_estimate=pl.CostEstimate(
            flops=4 * comps * depth * span_z * half * size_m * size_m, bytes_accessed=4 * own.size, transcendentals=0
        ),
    )(counts, oth_counts, mode_index, own, oth, own_w, oth_w, *extra)

    acc, edge = lax.optimization_barrier((acc, edge))
    oth_edge = other(edge)
    seam_scratch = [
        pltpu.VMEM((half * size_m, comps * depth), jnp.bfloat16),
        pltpu.VMEM((comps * depth, size_m), jnp.bfloat16),
        pltpu.VMEM((span_x, LANES, LANES), jnp.float32),
    ]
    acc = pl.pallas_call(
        functools.partial(seam_kernel, half, span_x, comps, False),
        out_shape=jax.ShapeDtypeStruct(acc.shape, jnp.float32),
        in_specs=[smem] + [vmem] * 3,
        out_specs=vmem,
        scratch_shapes=seam_scratch,
        compiler_params=params,
        cost_estimate=pl.CostEstimate(
            flops=4 * comps * depth * half * size_m * size_m, bytes_accessed=4 * own.size, transcendentals=0
        ),
    )(mode_index, acc, edge, last)
    partial = pl.pallas_call(
        functools.partial(seam_kernel, half, span_x, comps, True),
        out_shape=jax.ShapeDtypeStruct((size_gz, half * owned, size_m), jnp.bfloat16),
        in_specs=[smem] + [vmem] * 3,
        out_specs=vmem,
        scratch_shapes=seam_scratch + [pltpu.VMEM(acc.shape, jnp.float32)],
        compiler_params=params,
    )(mode_index, acc, oth_edge, oth_last)

    pieces = lax.all_to_all(partial, "gz", 0, 0, tiled=True)
    mine = pieces.astype(jnp.float32).sum(axis=0)
    if wrapped:
        theirs = other(mine)
        both = jnp.where(parity == 0, jnp.stack([mine, theirs]), jnp.stack([theirs, mine]))
    else:
        both = lax.psum(jnp.where(jnp.arange(2)[:, None, None] == parity, mine[None], 0.0), "gx")
    return both.reshape(window, owned, size_m)


def solution(mesh):
    placed = (P(None, "gx", None, "gz", None), P("gx", None, "gz"), P(("gx", "gz")), P())
    return jax.shard_map(
        local, mesh=mesh, in_specs=placed, out_specs=P(None, "gz", None), check_vma=False
    )
```

```python
import functools

import jax
import jax.numpy as jnp
from jax import lax
from jax.experimental import pallas as pl
from jax.experimental.pallas import tpu as pltpu
from jax.sharding import PartitionSpec as P

LANES = 128
PACKED = 16
GROUP = 2
SPLITS = 3
VMEM_LIMIT = 48 * 1024 * 1024


def pick_matrix(index_ref, half, comps, size_m):
    offset = (lax.axis_index("gx") % 2) * half
    lane = lax.broadcasted_iota(jnp.int32, (1, LANES), 1)
    target = jnp.full((1, LANES), -1, jnp.int32)
    for d in range(comps):
        for j in range(half):
            target = jnp.where(lane == d * half + j, index_ref[offset + j] + d * size_m, target)
    row = lax.broadcasted_iota(jnp.int32, (comps * size_m, LANES), 0)
    return jnp.where(row == target, 0.5, 0.0).astype(jnp.bfloat16)


def split_parts(value):
    parts = []
    for _ in range(SPLITS):
        part = value.astype(jnp.bfloat16)
        parts.append(part)
        value = value - part.astype(jnp.float32)
    return parts


def pack_kernel(own_ref, weight_ref, row_ref, first_ref, last_ref, near_ref, wide_ref, sems):
    comps, span_x, rows, size_m = own_ref.shape
    span_z, cap = weight_ref.shape[1:]
    depth = span_x * cap
    planes = [(c, x) for c in range(comps) for x in range(span_x)]
    copies = []
    for n, (c, x) in enumerate(planes):
        copy = pltpu.make_async_copy(own_ref.at[c, x], near_ref.at[c, x], sems.at[n])
        copy.start()
        copies.append(copy)
    spread = (
        lax.broadcasted_iota(jnp.int32, (cap, rows), 0) == lax.broadcasted_iota(jnp.int32, (cap, rows), 1) // span_z
    ).astype(jnp.bfloat16)
    column = lax.broadcasted_iota(jnp.int32, (span_z, rows), 1) % span_z
    mine = column == lax.broadcasted_iota(jnp.int32, (span_z, rows), 0)
    firsts, lasts = [], []
    for x in range(span_x):
        parts = split_parts(weight_ref[x])
        wide = jnp.dot(jnp.concatenate(parts, axis=0), spread, preferred_element_type=jnp.float32)
        total = wide[:span_z]
        for s in range(1, SPLITS):
            total = total + wide[s * span_z : (s + 1) * span_z]
        row_ref[x] = jnp.sum(jnp.where(mine, total, 0.0), axis=0, keepdims=True)
        firsts += [part[:1] for part in parts]
        lasts += [part[span_z - 1 :] for part in parts]
    filler = jnp.zeros((PACKED - SPLITS * span_x, cap), jnp.bfloat16)
    for out_ref, pieces in ((first_ref, firsts), (last_ref, lasts)):
        out_ref[comps * depth :, :] = jnp.concatenate(pieces + [filler], axis=0)
    for copy, (c, x) in zip(copies, planes):
        copy.wait()
        wide_ref[c, x] = near_ref[c, x].astype(jnp.float32)
        start = c * depth + x * cap
        for out_ref, z in ((first_ref, 0), (last_ref, span_z - 1)):
            out_ref[start : start + cap, :] = wide_ref[c, x, pl.ds(z, cap, stride=span_z), :].astype(jnp.bfloat16)


def main_kernel(wrapped, half, span_z, own_live_ref, oth_live_ref, index_ref, own_ref, oth_ref, own_w_ref, oth_w_ref, *rest):
    edges = () if wrapped else rest[:2]
    acc_ref, pick_out_ref, pick_ref, picked_ref, grad_ref, low_ref, high_ref, test_ref, next_ref = rest[-9:]
    comps, span_x, rows, size_m = own_ref.shape
    part = LANES
    levels = part // span_z
    depth = span_x * part
    margin = 2 * span_z
    middle = half // 2
    refs = (own_ref, oth_ref)
    weights = (own_w_ref, oth_w_ref)
    column = lax.broadcasted_iota(jnp.int32, (1, span_z, size_m), 1)

    def neighbours(which, x):
        body, other = refs[which], refs[1 - which]
        if x > 0:
            low = (body, x - 1)
        else:
            low = (other, span_x - 1) if wrapped else (edges[which], 0)
        if x < span_x - 1:
            high = (body, x + 1)
        else:
            high = (other, 0) if wrapped else (edges[which], 1)
        return low, high

    def prepare(which, block):
        body = refs[which]
        base = pl.multiple_of(block * part, part)
        spot = pl.ds(base, part)
        before = pl.ds(pl.multiple_of(jnp.maximum(base - margin, 0), margin), margin)
        after = pl.ds(pl.multiple_of(jnp.minimum(base + part, rows - margin), margin), margin)
        wide = [jnp.concatenate([body[d, x, spot] for d in range(comps)], axis=1) for x in range(span_x)]
        picked = jnp.dot(jnp.concatenate(wide, axis=0), pick_ref[...], preferred_element_type=jnp.float32)
        for x in range(span_x):
            weight = jnp.broadcast_to(weights[which][x, :, spot], (part, part)).T
            low, high = neighbours(which, x)
            for c in range(comps):
                mid = body[c, x, spot].astype(jnp.float32)
                row = c * depth + x * part
                next_ref[row : row + part, :] = (mid * weight).astype(jnp.bfloat16)
                gx = high[0][c, high[1], spot].astype(jnp.float32) - low[0][c, low[1], spot].astype(jnp.float32)
                grad_ref[x, c] = gx.T
                down = jnp.where(base > 0, body[c, x, before].astype(jnp.float32)[margin - span_z :], 0.0)
                up = jnp.where(base + part < rows, body[c, x, after].astype(jnp.float32)[:span_z], 0.0)
                gy = jnp.concatenate([mid[span_z:], up], axis=0) - jnp.concatenate([down, mid[: part - span_z]], axis=0)
                grad_ref[x, comps + c] = gy.T
                mid = mid.reshape(levels, span_z, size_m)
                right = jnp.where(column == span_z - 1, 0.0, pltpu.roll(mid, span_z - 1, 1))
                left = jnp.where(column == 0, 0.0, pltpu.roll(mid, 1, 1))
                grad_ref[x, 2 * comps + c] = (right - left).reshape(part, size_m).T
        for x in range(span_x):
            picked_ref[x] = picked[x * part : (x + 1) * part].T

    def advect(first, last, adv_ref):
        for j0 in range(first, last, GROUP):
            group = range(j0, min(j0 + GROUP, last))
            u = [
                [
                    [jnp.broadcast_to(picked_ref[x, d * half + j : d * half + j + 1, :], (PACKED, part)) for d in range(3)]
                    for x in range(span_x)
                ]
                for j in group
            ]
            for k in range(0, size_m, PACKED):
                for c in range(comps):
                    g = [[grad_ref[x, d * comps + c, k : k + PACKED, :] for d in range(3)] for x in range(span_x)]
                    for t, j in enumerate(group):
                        value = jnp.concatenate(
                            [u[t][x][0] * g[x][0] + u[t][x][1] * g[x][1] + u[t][x][2] * g[x][2] for x in range(span_x)],
                            axis=1,
                        )
                        row = (j - first) * size_m + k
                        adv_ref[row : row + PACKED, c * depth : (c + 1) * depth] = value.astype(jnp.bfloat16)

    def contract(first, last, adv_ref):
        some = slice(first * size_m, last * size_m)
        acc_ref[some, :] += jnp.dot(adv_ref[...], test_ref[...], preferred_element_type=jnp.float32)

    pick_ref[...] = pick_matrix(index_ref, half, comps, size_m)
    pick_out_ref[...] = pick_ref[(comps - 1) * size_m :, :]
    acc_ref[...] = jnp.zeros_like(acc_ref)
    test_ref[...] = jnp.zeros_like(test_ref)
    high_ref[...] = jnp.zeros_like(high_ref)
    def block_step(ahead):
        contract(middle, half, high_ref)
        advect(0, middle, low_ref)
        test_ref[...] = next_ref[...]
        contract(0, middle, low_ref)
        advect(middle, half, high_ref)
        if ahead is not None:
            prepare(*ahead)

    def blocks_but_last(which, live_ref):
        def step(block, carry):
            block_step((which, block + 1))
            return carry

        lax.fori_loop(0, pl.cdiv(live_ref[0], levels) - 1, step, 0)

    prepare(0, 0)
    blocks_but_last(0, own_live_ref)
    block_step((1, 0))
    blocks_but_last(1, oth_live_ref)
    block_step(None)
    contract(middle, half, high_ref)


def seam_kernel(half, span_x, comps, final, pick_ref, acc_ref, edge_ref, last_ref, out_ref, adv_ref, test_ref, picked_ref, *rest):
    size_m = acc_ref.shape[1]
    part = LANES
    depth = span_x * part
    body = comps * depth
    total_ref = rest[0] if final else out_ref
    pick = pick_ref[...]
    update = acc_ref[...]
    for tested_ref, field_ref, sign in ((last_ref, edge_ref, 1.0), (edge_ref, last_ref, -1.0)):
        third = tested_ref[(comps - 1) * depth : body, :]
        picked = sign * jnp.dot(third, pick, preferred_element_type=jnp.float32)
        splits = tested_ref[body:, :].astype(jnp.float32)
        for x in range(span_x):
            row = sum(splits[x * SPLITS + s : x * SPLITS + s + 1] for s in range(SPLITS))
            weight = jnp.broadcast_to(row, (part, part)).T
            picked_ref[x] = picked[x * part : (x + 1) * part].T
            for c in range(comps):
                spot = slice(c * depth + x * part, c * depth + (x + 1) * part)
                test_ref[spot, :] = (tested_ref[spot, :].astype(jnp.float32) * weight).astype(jnp.bfloat16)
        for c in range(comps):
            spots = [slice(c * depth + x * part, c * depth + (x + 1) * part) for x in range(span_x)]
            fields = [field_ref[spot, :].astype(jnp.float32).T for spot in spots]
            for j in range(half):
                lane = (comps - 1) * half + j
                value = jnp.concatenate([fields[x] * picked_ref[x, lane : lane + 1, :] for x in range(span_x)], axis=1)
                adv_ref[j * size_m : (j + 1) * size_m, c * depth : (c + 1) * depth] = value.astype(jnp.bfloat16)
        update = update + jnp.dot(adv_ref[...], test_ref[...], preferred_element_type=jnp.float32)
        total_ref[...] = update
        update = total_ref[...]
    if final:
        pieces = out_ref.shape[0]
        owned = size_m // pieces
        group = max(1, PACKED // owned)
        for j0 in range(0, half, group):
            parts = [
                total_ref[j * size_m : (j + 1) * size_m, :].T.reshape(pieces, owned, size_m)
                for j in range(j0, j0 + group)
            ]
            out_ref[:, j0 * owned : (j0 + group) * owned, :] = jnp.concatenate(parts, axis=1).astype(jnp.bfloat16)


def local(modes, weights, counts, mode_index):
    comps, span_x, cap, span_z, size_m = modes.shape
    size_gx, size_gz = lax.axis_size("gx"), lax.axis_size("gz")
    window = mode_index.shape[0]
    half = window // 2
    rows = cap * span_z
    depth = span_x * cap
    owned = size_m // size_gz
    wrapped = size_gx == 2
    parity = lax.axis_index("gx") % 2
    swap = [(i, i ^ 1) for i in range(size_gx)]
    leftward = [(i, (i - 1) % size_gz) for i in range(size_gz)]
    vmem = pl.BlockSpec(memory_space=pltpu.VMEM)
    smem = pl.BlockSpec(memory_space=pltpu.SMEM)
    anywhere = pl.BlockSpec(memory_space=pltpu.HBM)
    params = pltpu.CompilerParams(vmem_limit_bytes=VMEM_LIMIT)

    def other(value):
        return lax.ppermute(value, "gx", swap)

    own = modes.reshape(comps, span_x, rows, size_m)
    oth = other(own)
    oth_counts = other(counts)
    extra = []
    if not wrapped:
        low = lax.ppermute(own[:, -1:], "gx", [(i, (i + 1) % size_gx) for i in range(size_gx)])
        high = lax.ppermute(own[:, :1], "gx", [(i, (i - 1) % size_gx) for i in range(size_gx)])
        own_edge = jnp.concatenate([low, high], axis=1)
        extra = [own_edge, other(own_edge)]

    masked = jnp.where(jnp.arange(cap) < counts[0], weights.transpose(0, 2, 1), 0.0)
    column = jax.ShapeDtypeStruct((comps * depth + PACKED, size_m), jnp.bfloat16)
    own_w, first, last = pl.pallas_call(
        pack_kernel,
        out_shape=[jax.ShapeDtypeStruct((span_x, 1, rows), jnp.float32), column, column],
        in_specs=[anywhere, vmem],
        out_specs=[vmem] * 3,
        scratch_shapes=[
            pltpu.VMEM((comps, span_x, rows, size_m), jnp.bfloat16),
            pltpu.VMEM((comps, span_x, rows, size_m), jnp.float32),
            pltpu.SemaphoreType.DMA((comps * span_x,)),
        ],
        compiler_params=params,
    )(own, masked)
    edge = lax.ppermute(first, "gz", leftward)
    oth_w = other(own_w)
    oth_last = other(last)

    block_depth = comps * span_x * LANES
    acc, pick = pl.pallas_call(
        functools.partial(main_kernel, wrapped, half, span_z),
        out_shape=[
            jax.ShapeDtypeStruct((half * size_m, size_m), jnp.float32),
            jax.ShapeDtypeStruct((size_m, LANES), jnp.bfloat16),
        ],
        in_specs=[smem] * 3 + [vmem] * (4 + len(extra)),
        out_specs=[vmem] * 2,
        scratch_shapes=[
            pltpu.VMEM((comps * size_m, LANES), jnp.bfloat16),
            pltpu.VMEM((span_x, LANES, LANES), jnp.float32),
            pltpu.VMEM((span_x, 3 * comps, size_m, LANES), jnp.float32),
            pltpu.VMEM((half // 2 * size_m, block_depth), jnp.bfloat16),
            pltpu.VMEM(((half - half // 2) * size_m, block_depth), jnp.bfloat16),
            pltpu.VMEM((block_depth, size_m), jnp.bfloat16),
            pltpu.VMEM((block_depth, size_m), jnp.bfloat16),
        ],
        compiler_params=params,
        cost_estimate=pl.CostEstimate(
            flops=4 * comps * depth * span_z * half * size_m * size_m, bytes_accessed=4 * own.size, transcendentals=0
        ),
    )(counts, oth_counts, mode_index, own, oth, own_w, oth_w, *extra)

    acc, edge = lax.optimization_barrier((acc, edge))
    oth_edge = other(edge)
    seam_scratch = [
        pltpu.VMEM((half * size_m, comps * depth), jnp.bfloat16),
        pltpu.VMEM((comps * depth, size_m), jnp.bfloat16),
        pltpu.VMEM((span_x, LANES, LANES), jnp.float32),
    ]
    acc = pl.pallas_call(
        functools.partial(seam_kernel, half, span_x, comps, False),
        out_shape=jax.ShapeDtypeStruct(acc.shape, jnp.float32),
        in_specs=[vmem] * 4,
        out_specs=vmem,
        scratch_shapes=seam_scratch,
        compiler_params=params,
        cost_estimate=pl.CostEstimate(
            flops=4 * comps * depth * half * size_m * size_m, bytes_accessed=4 * own.size, transcendentals=0
        ),
    )(pick, acc, edge, last)
    partial = pl.pallas_call(
        functools.partial(seam_kernel, half, span_x, comps, True),
        out_shape=jax.ShapeDtypeStruct((size_gz, half * owned, size_m), jnp.bfloat16),
        in_specs=[vmem] * 4,
        out_specs=vmem,
        scratch_shapes=seam_scratch + [pltpu.VMEM(acc.shape, jnp.float32)],
        compiler_params=params,
    )(pick, acc, oth_edge, oth_last)

    pieces = lax.all_to_all(partial, "gz", 0, 0, tiled=True)
    mine = pieces.astype(jnp.float32).sum(axis=0)
    if wrapped:
        theirs = other(mine)
        both = jnp.where(parity == 0, jnp.stack([mine, theirs]), jnp.stack([theirs, mine]))
    else:
        both = lax.psum(jnp.where(jnp.arange(2)[:, None, None] == parity, mine[None], 0.0), "gx")
    return both.reshape(window, owned, size_m)


def solution(mesh):
    placed = (P(None, "gx", None, "gz", None), P("gx", None, "gz"), P(("gx", "gz")), P())
    return jax.shard_map(
        local, mesh=mesh, in_specs=placed, out_specs=P(None, "gz", None), check_vma=False
    )
```
